256 devices in a mesh: wide: 64 (over z, x, core), narrow: 4 (over y).
Axes of the slice: x: 4, y: 4, z: 8, core: 2. Of those that a mesh axis runs over, the one named last changes fastest.
Arguments:
- raw_record: bfloat16 [4, 32768, 8192], P('narrow', 'wide'), may hold values from -600 to 600
- filter_taps: bfloat16 [32], replicated, may hold values from -1 to 1
- health_mask: int32 [8192], replicated, may hold values from 0 to 1, as said below
- counts: int32 [64], replicated, may hold values from 8 to 64, as said below
- source_index: int32 [64], replicated, may hold values from 0 to 8191, as said below
Outputs:
- correlations: float32 [64, 8192, 256], P('narrow', 'wide')
The draws below stay inside these ranges and needn't reach their ends.
Inputs may be any that keep to these rules, and one draw needn't show every extreme that they name: `health_mask`: the first channel of each block and every source channel are flagged 1. Block b's channels on the fibre are the counts[b] leading ones, b * 128 to b * 128 + counts[b] - 1; some block has exactly 64. `source_index`: every source channel lies on the fibre and is healthy; two sources may coincide.
All inputs are finite; a program needn't handle non-finite values.
Results may differ from the reference program's by a relative error of at most 0.013.
Values may be sent and summed in bfloat16 or wider, within the bound.
A program may use at most 128 MiB of HBM per device.

```python
import math
import jax
import jax.numpy as jnp
from jax import lax

C = 8192
BLOCK_CH = 128
CAP = 64
Q = 2
L = 256
F = 128
K = 32
SRC = 64
SUBWIN = 4
TIME_SUB = 32768


def live_layout(key):
    count_key, big_key, block_key, slot_key, health_key = jax.random.split(key, 5)
    block_total = C // BLOCK_CH
    counts = jax.random.randint(count_key, (block_total,), CAP // 8, CAP + 1, dtype=jnp.int32)
    counts = counts.at[jax.random.randint(big_key, (), 0, block_total, dtype=jnp.int32)].set(CAP)
    src_block = jax.random.randint(block_key, (SRC,), 0, block_total, dtype=jnp.int32)
    src_slot = jax.random.randint(slot_key, (SRC,), 0, counts[src_block], dtype=jnp.int32)
    sources = src_block * BLOCK_CH + src_slot
    health = (jax.random.randint(health_key, (C,), 0, 20, dtype=jnp.int32) >= 3).astype(jnp.int32)
    health = health.at[jnp.arange(block_total, dtype=jnp.int32) * BLOCK_CH].set(1)
    health = health.at[sources].set(1)
    return (health, counts, sources)


def draw_health_mask(key, part):
    shared = live_layout(key)
    return shared[0]


def draw_counts(key, part):
    shared = live_layout(key)
    return shared[1]


def draw_source_index(key, part):
    shared = live_layout(key)
    return shared[2]


def draw_raw_record(key, part):
    key = jax.random.fold_in(key, 11)
    noise_key, gain_key, envelope_key = jax.random.split(key, 3)
    gains = jnp.exp(jax.random.uniform(gain_key, (1, 1, C), jnp.float32, 0.0, math.log(10.0)))
    envelope = jnp.exp(jax.random.uniform(envelope_key, (SUBWIN, TIME_SUB, 1), jnp.float32, 0.0, math.log(10.0)))
    random_noise = jnp.clip(jax.random.normal(noise_key, (SUBWIN, TIME_SUB, C), jnp.float32), -6.0, 6.0)
    return (random_noise * envelope * gains).astype(jnp.bfloat16)


def scatter_about(key, shape, deviation, most, held_as=jnp.bfloat16):
    result = jax.random.normal(key, shape, jnp.float32) * deviation
    return jnp.minimum(jnp.maximum(result, -most), most).astype(held_as)


def setup_inputs(seed: int = 0) -> dict:
    key_of = jax.random.split(jax.random.key(seed), 6)
    return {
        "raw_record": draw_raw_record(jax.random.fold_in(key_of[5], 71), 0),
        "filter_taps": scatter_about(key_of[1], (K,), K ** -0.5, 1.0),
        "health_mask": draw_health_mask(jax.random.fold_in(key_of[5], 71), 0),
        "counts": draw_counts(jax.random.fold_in(key_of[5], 71), 0),
        "source_index": draw_source_index(jax.random.fold_in(key_of[5], 71), 0),
    }


def taps_matrix(filter_taps, row_count, factor_q):
    tap_count = filter_taps.shape[0]
    columns = tap_count - factor_q + factor_q * row_count
    row_ids = jnp.arange(row_count, dtype=jnp.int32)[:, None]
    col_ids = jnp.arange(columns, dtype=jnp.int32)[None, :]
    offset = tap_count - 1 + factor_q * row_ids - col_ids
    selector = (offset[:, :, None] == jnp.arange(tap_count, dtype=jnp.int32)[None, None, :]).astype(jnp.float32)
    return lax.optimization_barrier(jnp.sum(selector * filter_taps.astype(jnp.float32)[None, None, :], axis=2)).astype(jnp.bfloat16)

def dft_table(length, bin_count):
    freq_ids = jnp.arange(1, bin_count + 1, dtype=jnp.int32)[:, None]
    sample_ids = jnp.arange(length, dtype=jnp.int32)[None, :]
    phases = freq_ids * sample_ids % length
    angles = phases.astype(jnp.float32) * (2.0 * math.pi / length)
    return jnp.concatenate([jnp.cos(angles), -jnp.sin(angles)], axis=0).astype(jnp.bfloat16)

def lag_table(length, bin_count):
    freq_ids = jnp.arange(1, bin_count + 1, dtype=jnp.int32)[:, None]
    lag_ids = jnp.arange(length, dtype=jnp.int32)[None, :] - length // 2
    phases = freq_ids * lag_ids % length
    angles = phases.astype(jnp.float32) * (2.0 * math.pi / length)
    return jnp.stack([jnp.cos(angles), -jnp.sin(angles)], axis=0).astype(jnp.bfloat16)

def live_flags(health_mask, counts, block_width):
    slot_ids = jnp.arange(block_width, dtype=jnp.int32)[None, :]
    inside = (counts[:, None] > slot_ids).astype(jnp.int32).reshape(-1)
    return health_mask * inside

def spectrum(extended, matrix_taps, table_dft, weights):
    decimated = jnp.dot(matrix_taps, extended, preferred_element_type=jnp.float32)
    scaling = lax.rsqrt(lax.optimization_barrier(jnp.mean(decimated * decimated, axis=0)) + 1e-06)
    normed = (decimated * scaling[None, :]).astype(jnp.bfloat16)
    spectra = jnp.dot(table_dft, normed, preferred_element_type=jnp.float32)
    bin_count = spectra.shape[0] // 2
    powers = spectra[:bin_count] * spectra[:bin_count] + spectra[bin_count:] * spectra[bin_count:]
    levels = jnp.dot(powers, weights, precision=lax.Precision.HIGHEST) / jnp.sum(weights) + 1e-06
    inverse = lax.rsqrt(levels)
    return (spectra * jnp.concatenate([inverse, inverse])[:, None]).astype(jnp.bfloat16)

def cross_terms(sources, channels):
    turned = jnp.stack([-sources[:, 1], sources[:, 0]], axis=1)
    wide_chan = channels.astype(jnp.float32)
    real_part = jnp.einsum('spfk,spfc->kfc', sources.astype(jnp.float32), wide_chan, precision=lax.Precision.HIGHEST)
    imag_part = jnp.einsum('spfk,spfc->kfc', turned.astype(jnp.float32), wide_chan, precision=lax.Precision.HIGHEST)
    return jnp.stack([real_part, imag_part], axis=1)

def reference(raw_record, filter_taps, health_mask, counts, source_index):
    living = live_flags(health_mask, counts, BLOCK_CH)
    weights = living.astype(jnp.float32)
    matrix_taps = taps_matrix(filter_taps, L, Q)
    table_dft = dft_table(L, F)
    table_lag = lag_table(L, F)
    margin = K - Q
    segments = TIME_SUB // (Q * L)

    def window_spectra(series):
        padded = jnp.concatenate([jnp.zeros((margin, C), jnp.bfloat16), series], axis=0)

        def segment(position):
            extended = lax.dynamic_slice_in_dim(padded, position * (Q * L), Q * L + margin, 0)
            return spectrum(extended, matrix_taps, table_dft, weights)
        return lax.map(segment, jnp.arange(segments, dtype=jnp.int32))
    spectra = lax.map(window_spectra, raw_record)
    sources = jnp.take(spectra, source_index, axis=3).reshape(SUBWIN, segments, 2, F, SRC)
    factor = 1.0 / math.sqrt(segments * SUBWIN * F)

    def block_lags(position):
        first = position * BLOCK_CH
        channels = lax.dynamic_slice_in_dim(spectra, first, BLOCK_CH, 3).reshape(SUBWIN, segments, 2, F, BLOCK_CH)
        stacked = jnp.zeros((SRC, 2, F, BLOCK_CH), jnp.float32)
        for window in range(SUBWIN):
            rounded = lax.optimization_barrier(cross_terms(sources[window], channels[window]).astype(jnp.bfloat16))
            stacked = stacked + rounded.astype(jnp.float32)
        chan_ids = first + jnp.arange(BLOCK_CH, dtype=jnp.int32)
        alive_cols = lax.dynamic_slice_in_dim(weights, first, BLOCK_CH, 0)
        distinct = (chan_ids[None, :] != source_index[:, None]).astype(jnp.float32)
        masked = (stacked * alive_cols[None, None, None, :] * distinct[:, None, None, :]).astype(jnp.bfloat16)
        return jnp.einsum('kpfc,pft->kct', masked.astype(jnp.float32), table_lag.astype(jnp.float32), precision=lax.Precision.HIGHEST) * factor
    blocks = lax.map(block_lags, jnp.arange(C // BLOCK_CH, dtype=jnp.int32))
    return jnp.transpose(blocks, (1, 0, 2, 3)).reshape(SRC, C, L)
```

```python
import functools
import math

import jax
import jax.numpy as jnp
import numpy as np
from jax import lax
from jax.experimental import pallas as pl
from jax.experimental.pallas import tpu as pltpu
from jax.sharding import PartitionSpec as P

C = 8192
BLOCK_CH = 128
CAP = 64
Q = 2
L = 256
F = 128
K = 32
SRC = 64
NZ, NX, NC, NY = 8, 4, 2, 4
WIDE = NZ * NX * NC
HALO = 32
CHUNKS = 4
FC = F // CHUNKS
GROUP = 16
SHARE = SRC // NY
STEPS = 16
STEP_RAW = C // STEPS
STEP_CH = STEP_RAW // 2
ROW = L * Q
MESH = pl.DeviceIdType.MESH
Z_ORDER = (4, 3, 5, 2, 6, 1, 7, 0)


def dft_table():
    phases = np.arange(1, F + 1)[:, None] * np.arange(L)[None, :] % L
    angles = phases.astype(np.float32) * np.float32(2.0 * math.pi / L)
    return np.concatenate([np.cos(angles), -np.sin(angles)], axis=0).astype(jnp.bfloat16)


def lag_table():
    phases = np.arange(1, F + 1)[:, None] * (np.arange(L)[None, :] - L // 2) % L
    angles = phases.astype(np.float32) * np.float32(2.0 * math.pi / L)
    return np.stack([np.cos(angles), -np.sin(angles)], axis=0).astype(jnp.bfloat16)


def lanes(shape):
    return lax.broadcasted_iota(jnp.int32, shape, len(shape) - 1)


def paired(even, odd):
    return jnp.where(lanes(even.shape) < CAP, even, pltpu.roll(odd, CAP, 1))


def step_pair(step, z):
    plane = step // 2
    distance = jnp.int32(Z_ORDER[-1])
    for i, d in enumerate(Z_ORDER[:-1]):
        distance = jnp.where(plane == i, jnp.int32(d), distance)
    return lax.rem(z + distance, NZ) * NX + lax.rem(step, 2) * 2


def spectra_kernel(
    raw, first_row, dft, weights, source_row, source_col, out,
    samples, edge, edge_out, edge_in, taps, decimated, level_acc, source_acc,
    outgoing, incoming, sources, chan_t, source_t, cross, parts,
    raw_sem, edge_sem, halo_send, halo_recv, send_sem, recv_sem,
    gather_send, gather_recv, y_send, y_recv,
):
    w = lax.axis_index("wide")
    y = lax.axis_index("narrow")
    z, x, core = w // (NX * NC), lax.rem(w // NC, NX), lax.rem(w, NC)

    edge_copy = pltpu.make_async_copy(raw.at[0, pl.ds(ROW - HALO, HALO)], edge, edge_sem)
    edge_copy.start()

    def raw_copy(step):
        at = pl.multiple_of(step_pair(step, z) * 2 * BLOCK_CH, STEP_RAW)
        return pltpu.make_async_copy(
            raw.at[0, :, pl.ds(at, STEP_RAW)], samples.at[step], raw_sem.at[step]
        )

    @pl.loop(0, STEPS)
    def _(step):
        raw_copy(step).start()

    barrier = pltpu.get_barrier_semaphore()

    @pl.loop(1, WIDE)
    def _(t):
        pl.semaphore_signal(
            barrier, inc=1, device_id=(lax.rem(w + t, WIDE), y), device_id_type=MESH
        )

    for t in range(1, NY):
        pl.semaphore_signal(
            barrier, inc=1, device_id=(w, lax.rem(y + t, NY)), device_id_type=MESH
        )

    circular = pltpu.roll(
        jnp.broadcast_to(first_row[0:1, :], (L, ROW)), 0, 1, stride=Q, stride_axis=0
    )
    rows = lax.broadcasted_iota(jnp.int32, (L, ROW), 0)
    inside = lanes((L, ROW)) <= Q * rows + 1
    taps[...] = jnp.where(inside, circular, 0.0).astype(jnp.bfloat16)
    halo_taps = jnp.where(inside[:16], 0.0, circular[:16])[:, ROW - BLOCK_CH :]
    halo_taps = pltpu.roll(jnp.where(w == 0, 0.0, halo_taps), HALO, 1)[:, :HALO]
    halo_taps = halo_taps.astype(jnp.bfloat16)

    edge_copy.wait()
    for b in range(C // BLOCK_CH // 2):
        at = 2 * b * BLOCK_CH
        pair = edge[:, at : at + 2 * BLOCK_CH].astype(jnp.float32)
        edge_out[:, b * BLOCK_CH : (b + 1) * BLOCK_CH] = paired(
            pair[:, :BLOCK_CH], pair[:, BLOCK_CH:]
        ).astype(jnp.bfloat16)

    pl.semaphore_wait(barrier, WIDE - 1 + NY - 1)
    halo = pltpu.make_async_remote_copy(
        src_ref=edge_out,
        dst_ref=edge_in,
        send_sem=halo_send,
        recv_sem=halo_recv,
        device_id=(lax.rem(w + 1, WIDE), y),
        device_id_type=MESH,
    )
    halo.start()

    level_acc[...] = jnp.zeros_like(level_acc)
    source_acc[...] = jnp.zeros_like(source_acc)

    @pl.loop(0, STEPS)
    def _(step):
        raw_copy(step).wait()
        d = jnp.dot(taps[...], samples[step], preferred_element_type=jnp.float32)
        for p in range(2):
            at = 2 * p * BLOCK_CH
            decimated[step, :, p * BLOCK_CH : (p + 1) * BLOCK_CH] = paired(
                d[:, at : at + BLOCK_CH], d[:, at + BLOCK_CH : at + 2 * BLOCK_CH]
            )

    halo.wait()

    def send(chunk, dest):
        return pltpu.make_async_remote_copy(
            src_ref=outgoing.at[chunk, dest],
            dst_ref=incoming.at[chunk, w],
            send_sem=send_sem.at[chunk],
            recv_sem=recv_sem.at[chunk],
            device_id=(dest, y),
            device_id_type=MESH,
        )

    def own(chunk):
        return pltpu.make_async_copy(
            outgoing.at[chunk, w], incoming.at[chunk, w], recv_sem.at[chunk]
        )

    def start_send(chunk, dest):
        @pl.when(dest != w)
        def _():
            send(chunk, dest).start()

        @pl.when(dest == w)
        def _():
            own(chunk).start()

    @pl.loop(0, STEPS)
    def _(step):
        first = step_pair(step, z)
        at = pl.multiple_of(first * BLOCK_CH, STEP_CH)
        head = jnp.dot(
            halo_taps,
            edge_in[:, pl.ds(at, STEP_CH)],
            preferred_element_type=jnp.float32,
        )
        d = decimated[step]
        d = jnp.concatenate([d[:16] + head, d[16:]], axis=0)
        scaling = lax.rsqrt(jnp.sum(d * d, axis=0, keepdims=True) * (1.0 / L) + 1e-06)
        normed = (d * scaling).astype(jnp.bfloat16)
        spectra = jnp.dot(dft[...], normed, preferred_element_type=jnp.float32)
        total = level_acc[...]
        for p in range(2):
            pair = first + p
            re = spectra[:F, p * BLOCK_CH : (p + 1) * BLOCK_CH]
            im = spectra[F:, p * BLOCK_CH : (p + 1) * BLOCK_CH]
            total = total + (re * re + im * im) * weights[pl.ds(pair, 1), :]
            low = lanes(re.shape) < CAP
            blocks = (
                jnp.where(low, re, pltpu.roll(im, CAP, 1)).astype(jnp.bfloat16),
                jnp.where(low, pltpu.roll(re, CAP, 1), im).astype(jnp.bfloat16),
            )
            for c in range(NC):
                for chunk in range(CHUNKS):
                    outgoing[chunk, 2 * pair + c] = blocks[c][chunk * FC : (chunk + 1) * FC]
        level_acc[...] = total
        for p in range(2):
            for c in range(NC):
                start_send(0, 2 * (first + p) + c)
        slots = lax.broadcasted_iota(jnp.int32, (STEP_CH, BLOCK_CH), 0)
        ids = (2 * first + slots // CAP) * BLOCK_CH + lax.rem(slots, CAP)
        chosen = (ids == source_row[...]).astype(jnp.float32).astype(jnp.bfloat16)
        source_acc[...] += jnp.dot(
            spectra.astype(jnp.bfloat16), chosen, preferred_element_type=jnp.float32
        )

    levels = jnp.sum(level_acc[...], axis=1, keepdims=True) / jnp.sum(weights[...]) + 1e-06
    picked = source_acc[...]
    picked = jnp.where(lanes((F, BLOCK_CH)) < SRC, picked[:F], picked[F:])
    sources[z, x, core] = (picked / levels).astype(jnp.bfloat16)

    def gather(phase, view, device):
        return pltpu.make_async_remote_copy(
            src_ref=view,
            dst_ref=view,
            send_sem=gather_send.at[phase],
            recv_sem=gather_recv.at[phase],
            device_id=(device, y),
            device_id_type=MESH,
        )

    def arrived(view, sem):
        pltpu.make_async_copy(view, view, sem).wait()

    def send_rest(chunk):
        @pl.loop(0, WIDE)
        def _(t):
            start_send(chunk, lax.rem(w + WIDE // 2 + t, WIDE))

    for t in range(1, NZ):
        to = (lax.rem(z + t, NZ) * NX + x) * NC + core
        gather(0, sources.at[z, x, core], to).start()
    send_rest(1)
    arrived(sources.at[pl.ds(0, NZ - 1), x, core], gather_recv.at[0])
    for t in range(1, NX):
        to = (z * NX + lax.rem(x + t, NX)) * NC + core
        gather(1, sources.at[:, x, core], to).start()
    send_rest(2)
    arrived(sources.at[:, pl.ds(0, NX - 1), core], gather_recv.at[1])
    gather(2, sources.at[:, :, core], w + 1 - 2 * core).start()
    send_rest(3)
    arrived(sources.at[:, :, 1 - core], gather_recv.at[2])

    def y_copy(chunk, to):
        return pltpu.make_async_remote_copy(
            src_ref=cross.at[chunk, to],
            dst_ref=parts.at[chunk, y],
            send_sem=y_send.at[chunk],
            recv_sem=y_recv.at[chunk],
            device_id=(w, to),
            device_id_type=MESH,
        )

    sign = jnp.where(lanes((SRC, BLOCK_CH)) < CAP, 1.0, -1.0)

    def cross_chunk(chunk):
        arrived(incoming.at[chunk], recv_sem.at[chunk])

        @pl.loop(0, FC // GROUP)
        def _(g):
            at = pl.multiple_of(g * GROUP, GROUP)
            full = pl.multiple_of(chunk * FC + g * GROUP, GROUP)
            for q in range(WIDE // GROUP):
                held = incoming[chunk, q * GROUP : (q + 1) * GROUP, pl.ds(at, GROUP), :]
                chan_t[:, q * GROUP : (q + 1) * GROUP, :] = jnp.swapaxes(held, 0, 1)
                held = sources[2 * q : 2 * q + 2, :, :, pl.ds(full, GROUP), :]
                held = held.reshape(GROUP, GROUP, BLOCK_CH)
                source_t[:, q * GROUP : (q + 1) * GROUP, :] = jnp.swapaxes(held, 0, 1)
            for f in range(GROUP):
                product = lax.dot_general(
                    source_t[f], chan_t[f], (((0,), (0,)), ((), ())),
                    preferred_element_type=jnp.float32,
                )
                both = product[:SRC] + sign * pltpu.roll(product[SRC:], CAP, 1)
                both = both.astype(jnp.bfloat16)
                for k in range(NY):
                    cross[chunk, k, at + f] = both[k * SHARE : (k + 1) * SHARE]

        for t in range(1, NY):
            y_copy(chunk, lax.rem(y + t, NY)).start()
        pltpu.make_async_copy(cross.at[chunk, y], parts.at[chunk, y], y_recv.at[chunk]).start()

    lane = lanes((1, BLOCK_CH))
    alive = weights[pl.ds(w // 2, 1), :]
    turned = pltpu.roll(alive, CAP, 1)
    alive = jnp.where((lane < CAP) == (core == 0), alive, turned)
    own_ids = source_col[pl.ds(pl.multiple_of(y * SHARE, SHARE), SHARE), :]
    distinct = (w * BLOCK_CH + lax.rem(lane, CAP)) != own_ids
    keep = jnp.where(distinct, alive, 0.0)

    def sum_chunk(chunk):
        arrived(parts.at[chunk], y_recv.at[chunk])

        @pl.loop(0, FC)
        def _(f):
            total = parts[chunk, 0, f].astype(jnp.float32)
            for n in range(1, NY):
                total = total + parts[chunk, n, f].astype(jnp.float32)
            out[chunk * FC + f] = (total * keep).astype(jnp.bfloat16)

    for chunk in range(CHUNKS):
        cross_chunk(chunk)
        if chunk >= 1:
            sum_chunk(chunk - 1)
    sum_chunk(CHUNKS - 1)

    for chunk in range(CHUNKS):
        arrived(outgoing.at[chunk, pl.ds(0, WIDE - 1)], send_sem.at[chunk])
        arrived(cross.at[chunk, pl.ds(0, NY - 1)], y_send.at[chunk])
    arrived(sources.at[pl.ds(0, NZ - 1), x, core], gather_send.at[0])
    arrived(sources.at[:, pl.ds(0, NX - 1), core], gather_send.at[1])
    arrived(sources.at[:, :, core], gather_send.at[2])


def masked_spectra(raw, first_row, dft, weights, source_row, source_col):
    bf16, f32 = jnp.bfloat16, jnp.float32
    dma = pltpu.SemaphoreType.DMA
    vmem = pl.BlockSpec(memory_space=pltpu.VMEM)
    return pl.pallas_call(
        spectra_kernel,
        out_shape=jax.ShapeDtypeStruct((F, SHARE, BLOCK_CH), bf16),
        in_specs=[pl.BlockSpec(memory_space=pl.ANY)] + [vmem] * 5,
        out_specs=vmem,
        scratch_shapes=[
            pltpu.VMEM((STEPS, ROW, STEP_RAW), bf16),
            pltpu.VMEM((HALO, C), bf16),
            pltpu.VMEM((HALO, C // 2), bf16),
            pltpu.VMEM((HALO, C // 2), bf16),
            pltpu.VMEM((L, ROW), bf16),
            pltpu.VMEM((STEPS, L, STEP_CH), f32),
            pltpu.VMEM((F, BLOCK_CH), f32),
            pltpu.VMEM((2 * F, BLOCK_CH), f32),
            pltpu.VMEM((CHUNKS, WIDE, FC, BLOCK_CH), bf16),
            pltpu.VMEM((CHUNKS, WIDE, FC, BLOCK_CH), bf16),
            pltpu.VMEM((NZ, NX, NC, F, BLOCK_CH), bf16),
            pltpu.VMEM((GROUP, WIDE, BLOCK_CH), bf16),
            pltpu.VMEM((GROUP, WIDE, BLOCK_CH), bf16),
            pltpu.VMEM((CHUNKS, NY, FC, SHARE, BLOCK_CH), bf16),
            pltpu.VMEM((CHUNKS, NY, FC, SHARE, BLOCK_CH), bf16),
            dma((STEPS,)),
            dma,
            dma,
            dma,
            dma((CHUNKS,)),
            dma((CHUNKS,)),
            dma((3,)),
            dma((3,)),
            dma((CHUNKS,)),
            dma((CHUNKS,)),
        ],
        compiler_params=pltpu.CompilerParams(
            collective_id=0, has_side_effects=True, vmem_limit_bytes=48 << 20
        ),
        name="masked_spectra",
    )(raw, first_row, dft, weights, source_row, source_col)


def lag_kernel(masked, table, out, by_source):
    step = pl.program_id(0)

    @pl.when(step == 0)
    def _():
        by_source[...] = jnp.swapaxes(masked[...], 0, 1)

    factor = 1.0 / math.sqrt(WIDE * NY * F)
    for k in range(out.shape[0]):
        turned = by_source[step * out.shape[0] + k].T
        out[k, :CAP] = factor * (
            jnp.dot(turned[:CAP], table[0], preferred_element_type=jnp.float32)
            + jnp.dot(turned[CAP:], table[1], preferred_element_type=jnp.float32)
        )
        out[k, CAP:] = jnp.zeros((BLOCK_CH - CAP, L), jnp.float32)


def correlations(masked, table):
    part = 4
    return pl.pallas_call(
        lag_kernel,
        grid=(SHARE // part,),
        out_shape=jax.ShapeDtypeStruct((SHARE, BLOCK_CH, L), jnp.float32),
        in_specs=[
            pl.BlockSpec((F, SHARE, BLOCK_CH), lambda i: (0, 0, 0)),
            pl.BlockSpec((2, F, L), lambda i: (0, 0, 0)),
        ],
        out_specs=pl.BlockSpec((part, BLOCK_CH, L), lambda i: (i, 0, 0)),
        scratch_shapes=[pltpu.VMEM((SHARE, F, BLOCK_CH), jnp.bfloat16)],
        compiler_params=pltpu.CompilerParams(vmem_limit_bytes=16 << 20),
        name="correlations",
    )(masked, table)


def body(raw_record, filter_taps, health_mask, counts, source_index):
    taps = filter_taps.astype(jnp.float32)
    first_row = jnp.concatenate(
        [taps[1::-1], jnp.zeros((ROW - K,), jnp.float32), taps[:1:-1]]
    )
    first_row = jnp.broadcast_to(first_row[None, :], (8, ROW))
    slots = jnp.arange(CAP, dtype=jnp.int32)[None, :]
    living = health_mask.reshape(C // BLOCK_CH, BLOCK_CH)[:, :CAP] * (counts[:, None] > slots)
    weights = living.astype(jnp.float32).reshape(WIDE // 2, 2 * CAP)
    source_row = jnp.concatenate([source_index, source_index])[None, :]
    source_col = jnp.broadcast_to(source_index[:, None], (SRC, BLOCK_CH))
    masked = masked_spectra(
        raw_record, first_row, jnp.asarray(dft_table()), weights, source_row, source_col
    )
    return correlations(masked, jnp.asarray(lag_table()))


def solution(mesh):
    placed = (P("narrow", "wide", None), P(), P(), P(), P())
    return jax.shard_map(
        body, mesh=mesh, in_specs=placed, out_specs=P("narrow", "wide", None), check_vma=False
    )
```

```python
import functools
import math

import jax
import jax.numpy as jnp
import numpy as np
from jax import lax
from jax.experimental import pallas as pl
from jax.experimental.pallas import tpu as pltpu
from jax.sharding import PartitionSpec as P

C = 8192
BLOCK_CH = 128
CAP = 64
Q = 2
L = 256
F = 128
K = 32
SRC = 64
NZ, NX, NC, NY = 8, 4, 2, 4
WIDE = NZ * NX * NC
HALO = 32
NXC = NX * NC
PLANE = NXC * NY
FC = F // NY
GROUP = 16
SHARE = SRC // NY
STEPS = NZ
STEP_RAW = C // STEPS
STEP_CH = STEP_RAW // 2
ROW = L * Q
MESH = pl.DeviceIdType.MESH
Z_ORDER = (4, 3, 5, 2, 6, 1, 7, 0)
GROUPS = ((0, 1), (1, 2), (3, 2), (5, 2), (7, 1))
HOPS = 7
TAIL = 8
TAILS = FC // TAIL


def dft_table():
    phases = np.arange(1, F + 1)[:, None] * np.arange(L)[None, :] % L
    angles = phases.astype(np.float32) * np.float32(2.0 * math.pi / L)
    return np.concatenate([np.cos(angles), -np.sin(angles)], axis=0).astype(jnp.bfloat16)


def lag_table():
    phases = np.arange(1, F + 1)[:, None] * (np.arange(L)[None, :] - L // 2) % L
    angles = phases.astype(np.float32) * np.float32(2.0 * math.pi / L)
    return np.stack([np.cos(angles), -np.sin(angles)], axis=0).astype(jnp.bfloat16)


def lanes(shape):
    return lax.broadcasted_iota(jnp.int32, shape, len(shape) - 1)


def paired(even, odd):
    return jnp.where(lanes(even.shape) < CAP, even, pltpu.roll(odd, CAP, 1))


def step_plane(step, z):
    distance = jnp.int32(Z_ORDER[-1])
    for i, d in enumerate(Z_ORDER[:-1]):
        distance = jnp.where(step == i, jnp.int32(d), distance)
    return lax.rem(z + distance, NZ)


def spectra_kernel(
    raw, filter_taps, dft_hbm, health_hbm, counts_hbm, index_hbm, out,
    dft, health, counts, source_index, small_sem,
    samples, edge, edge_out, edge_in, taps, tap_row, decimated, level_acc, weight_acc, source_acc,
    outgoing, incoming, source_out, source_in, source_t, chan_t, sums, right_in, left_in,
    masked, quarters,
    raw_sem, edge_sem, halo_send, halo_recv, send_sem, recv_sem, source_send, source_recv,
    right_send, right_recv, left_send, left_recv, y_send, y_recv,
):
    w = lax.axis_index("wide")
    y = lax.axis_index("narrow")
    z, xc = w // NXC, lax.rem(w, NXC)
    me = xc * NY + y

    def peer(t):
        other = lax.rem(me + t, PLANE)
        return other // NY, lax.rem(other, NY)

    edge_copy = pltpu.make_async_copy(raw.at[0, pl.ds(ROW - HALO, HALO)], edge, edge_sem)
    edge_copy.start()
    small = [
        pltpu.make_async_copy(src, dst, small_sem.at[i])
        for i, (src, dst) in enumerate(
            (
                (index_hbm, source_index),
                (counts_hbm, counts),
                (health_hbm, health),
                (dft_hbm, dft),
            )
        )
    ]
    for copy in small:
        copy.start()

    def raw_copy(step):
        at = pl.multiple_of(step_plane(step, z) * STEP_RAW, STEP_RAW)
        return pltpu.make_async_copy(
            raw.at[0, :, pl.ds(at, STEP_RAW)], samples.at[step], raw_sem.at[step]
        )

    @pl.loop(0, STEPS)
    def _(step):
        raw_copy(step).start()

    barrier = pltpu.get_barrier_semaphore()

    def greet(wide, narrow):
        pl.semaphore_signal(barrier, inc=1, device_id=(wide, narrow), device_id_type=MESH)

    z_right, z_left = lax.rem(w + NXC, WIDE), lax.rem(w + WIDE - NXC, WIDE)
    after, before = lax.rem(w + 1, WIDE), lax.rem(w + WIDE - 1, WIDE)
    for wide in (after, before, z_right, z_left):
        greet(wide, y)

    @pl.loop(1, PLANE)
    def _(t):
        to_xc, to_y = peer(t)
        greet(z * NXC + to_xc, to_y)

    edge_copy.wait()
    for b in range(C // BLOCK_CH // 2):
        at = 2 * b * BLOCK_CH
        pair = edge[:, at : at + 2 * BLOCK_CH].astype(jnp.float32)
        edge_out[:, b * BLOCK_CH : (b + 1) * BLOCK_CH] = paired(
            pair[:, :BLOCK_CH], pair[:, BLOCK_CH:]
        ).astype(jnp.bfloat16)

    pl.semaphore_wait(barrier, PLANE - 1 + 4)

    def halo(plane):
        columns = pl.ds(pl.multiple_of(plane * STEP_CH, STEP_CH), STEP_CH)
        return pltpu.make_async_remote_copy(
            src_ref=edge_out.at[:, columns],
            dst_ref=edge_in.at[:, columns],
            send_sem=halo_send.at[plane],
            recv_sem=halo_recv.at[plane],
            device_id=(after, y),
            device_id_type=MESH,
        )

    @pl.loop(0, STEPS)
    def _(step):
        halo(step_plane(step, z)).start()

    tap_row[...] = jnp.zeros_like(tap_row)
    tap_row[0:1, :K] = filter_taps[...].astype(jnp.float32)
    tap_ids = lax.broadcasted_iota(jnp.int32, (BLOCK_CH, ROW), 0)
    place = (lanes((BLOCK_CH, ROW)) + tap_ids == 1) | (lanes((BLOCK_CH, ROW)) + tap_ids == ROW + 1)
    first_row = jnp.dot(
        tap_row[...].astype(jnp.bfloat16),
        jnp.where(place, 1.0, 0.0).astype(jnp.bfloat16),
        preferred_element_type=jnp.float32,
    )
    circular = pltpu.roll(
        jnp.broadcast_to(first_row[0:1, :], (L, ROW)), 0, 1, stride=Q, stride_axis=0
    )
    rows = lax.broadcasted_iota(jnp.int32, (L, ROW), 0)
    inside = lanes((L, ROW)) <= Q * rows + 1
    taps[...] = jnp.where(inside, circular, 0.0).astype(jnp.bfloat16)
    halo_taps = jnp.where(inside[:16], 0.0, circular[:16])[:, ROW - BLOCK_CH :]
    halo_taps = pltpu.roll(jnp.where(w == 0, 0.0, halo_taps), HALO, 1)[:, :HALO]
    halo_taps = halo_taps.astype(jnp.bfloat16)

    lane = lanes((1, BLOCK_CH))
    slot_lane = lax.rem(lane, CAP)
    for copy in small:
        copy.wait()
    source_row = jnp.zeros((1, BLOCK_CH), jnp.int32)
    for k in range(SRC):
        source_row = jnp.where(slot_lane == k, source_index[k], source_row)

    level_acc[...] = jnp.zeros_like(level_acc)
    weight_acc[...] = jnp.zeros_like(weight_acc)
    source_acc[...] = jnp.zeros_like(source_acc)

    @pl.loop(0, STEPS)
    def _(step):
        raw_copy(step).wait()
        d = jnp.dot(taps[...], samples[step], preferred_element_type=jnp.float32)
        for p in range(NX):
            at = 2 * p * BLOCK_CH
            decimated[step, :, p * BLOCK_CH : (p + 1) * BLOCK_CH] = paired(
                d[:, at : at + BLOCK_CH], d[:, at + BLOCK_CH : at + 2 * BLOCK_CH]
            )

    def spectra_step(step):
        plane = step_plane(step, z)
        first = plane * NX
        at = pl.multiple_of(plane * STEP_CH, STEP_CH)
        halo(plane).wait_recv()
        head = jnp.dot(
            halo_taps, edge_in[:, pl.ds(at, STEP_CH)], preferred_element_type=jnp.float32
        )
        d = decimated[step]
        d = jnp.concatenate([d[:16] + head, d[16:]], axis=0)
        scaling = lax.rsqrt(jnp.sum(d * d, axis=0, keepdims=True) * (1.0 / L) + 1e-06)
        normed = (d * scaling).astype(jnp.bfloat16)
        spectra = jnp.dot(dft[...], normed, preferred_element_type=jnp.float32)
        total = level_acc[...]
        for p in range(NX):
            pair = first + p
            re = spectra[:F, p * BLOCK_CH : (p + 1) * BLOCK_CH]
            im = spectra[F:, p * BLOCK_CH : (p + 1) * BLOCK_CH]
            flags = paired(health[pl.ds(2 * pair, 1), :], health[pl.ds(2 * pair + 1, 1), :])
            count = jnp.where(lane < CAP, counts[2 * pair], counts[2 * pair + 1])
            weights = jnp.where(slot_lane < count, flags, 0).astype(jnp.float32)
            weight_acc[...] += weights
            total = total + (re * re + im * im) * weights
            low = lanes(re.shape) < CAP
            outgoing[step, 2 * p] = jnp.where(low, re, pltpu.roll(im, CAP, 1)).astype(jnp.bfloat16)
            outgoing[step, 2 * p + 1] = jnp.where(low, pltpu.roll(re, CAP, 1), im).astype(
                jnp.bfloat16
            )
        level_acc[...] = total
        slots = lax.broadcasted_iota(jnp.int32, (STEP_CH, BLOCK_CH), 0)
        ids = (2 * first + slots // CAP) * BLOCK_CH + lax.rem(slots, CAP)
        chosen = (ids == source_row).astype(jnp.float32).astype(jnp.bfloat16)
        source_acc[...] += jnp.dot(
            spectra.astype(jnp.bfloat16), chosen, preferred_element_type=jnp.float32
        )

    def bins(to_y):
        return pl.ds(pl.multiple_of(to_y * FC, FC), FC)

    def send_group(group):
        slots = pl.ds(*GROUPS[group])

        @pl.loop(1, PLANE)
        def _(t):
            to_xc, to_y = peer(t)
            pltpu.make_async_remote_copy(
                src_ref=outgoing.at[slots, to_xc, bins(to_y)],
                dst_ref=incoming.at[slots, me],
                send_sem=send_sem.at[group],
                recv_sem=recv_sem.at[group],
                device_id=(z * NXC + to_xc, to_y),
                device_id_type=MESH,
            ).start()

        pltpu.make_async_copy(
            outgoing.at[slots, xc, bins(y)], incoming.at[slots, me], recv_sem.at[group]
        ).start()

    def arrived(view, sem):
        pltpu.make_async_copy(view, view, sem).wait()

    spectra_step(0)
    send_group(0)

    @pl.loop(1, STEPS)
    def _(step):
        spectra_step(step)

    levels = jnp.sum(level_acc[...], axis=1, keepdims=True) / jnp.sum(weight_acc[...]) + 1e-06
    picked = source_acc[...]
    picked = jnp.where(lanes((F, BLOCK_CH)) < SRC, picked[:F], picked[F:])
    source_out[...] = (picked / levels).astype(jnp.bfloat16)

    @pl.loop(1, PLANE)
    def _(t):
        to_xc, to_y = peer(t)
        pltpu.make_async_remote_copy(
            src_ref=source_out.at[bins(to_y)],
            dst_ref=source_in.at[me],
            send_sem=source_send,
            recv_sem=source_recv,
            device_id=(z * NXC + to_xc, to_y),
            device_id_type=MESH,
        ).start()

    pltpu.make_async_copy(source_out.at[bins(y)], source_in.at[me], source_recv).start()
    send_group(1)

    def by_bin(held, turned):
        for f in range(FC // GROUP):
            for q in range(PLANE // GROUP):
                turned[f * GROUP : (f + 1) * GROUP, q * GROUP : (q + 1) * GROUP, :] = jnp.swapaxes(
                    held[q * GROUP : (q + 1) * GROUP, f * GROUP : (f + 1) * GROUP, :], 0, 1
                )

    arrived(source_in, source_recv)
    by_bin(source_in, source_t)
    sign = jnp.where(lanes((SRC, BLOCK_CH)) < CAP, 1.0, -1.0)

    def cross_slots(group):
        first, number = GROUPS[group]
        arrived(incoming.at[pl.ds(first, number)], recv_sem.at[group])
        for slot in range(first, first + number):
            by_bin(incoming.at[slot], chan_t)

            @pl.loop(0, FC // 8)
            def _(g, slot=slot):
                for i in range(8):
                    f = g * 8 + i
                    product = lax.dot_general(
                        source_t[f], chan_t[f], (((0,), (0,)), ((), ())),
                        preferred_element_type=jnp.float32,
                    )
                    both = product[:SRC] + sign * pltpu.roll(product[SRC:], CAP, 1)
                    both = both.astype(jnp.bfloat16)
                    for k in range(NY):
                        sums[slot, k, f] = both[k * SHARE : (k + 1) * SHARE]

    right = ((0, 0), (1, 1), (1, 0), (3, 1), (3, 0), (5, 1), (5, 0))
    left = ((0, 1), (2, 0), (2, 1), (4, 0), (4, 1), (6, 0), (6, 1))

    def half(slot, part):
        return sums.at[slot, pl.ds(2 * part, 2)]

    def tail(ref, i):
        return ref.at[:, pl.ds(i * TAIL, TAIL)]

    def add_in(slot, part, landed):
        @pl.loop(0, FC)
        def _(f):
            for k in range(2):
                both = sums[slot, 2 * part + k, f].astype(jnp.float32)
                both = both + landed[k, f].astype(jnp.float32)
                sums[slot, 2 * part + k, f] = both.astype(jnp.bfloat16)

    def forward(m):
        for route, landed, sends, recvs, to in (
            (right, right_in, right_send, right_recv, z_right),
            (left, left_in, left_send, left_recv, z_left),
        ):
            slot, part = route[m]
            if m >= 2:
                arrived(landed.at[m - 2], recvs.at[m - 2])
                add_in(slot, part, landed.at[m - 2])
            if m < HOPS - 1:
                pieces = [(half(slot, part), landed.at[m], m)]
            else:
                pieces = [
                    (tail(half(slot, part), i), tail(landed.at[m], i), m + i) for i in range(TAILS)
                ]
            for src, dst, sem in pieces:
                pltpu.make_async_remote_copy(
                    src_ref=src,
                    dst_ref=dst,
                    send_sem=sends.at[sem],
                    recv_sem=recvs.at[sem],
                    device_id=(to, y),
                    device_id_type=MESH,
                ).start()

    cross_slots(0)
    forward(0)
    send_group(2)
    cross_slots(1)
    forward(1)
    forward(2)
    send_group(3)
    send_group(4)
    cross_slots(2)
    forward(3)
    forward(4)
    cross_slots(3)
    forward(5)
    forward(6)
    cross_slots(4)

    alive = jnp.where(slot_lane < counts[w], health[pl.ds(w, 1), :], 0)
    alive = jnp.where(lane < CAP, alive, pltpu.roll(alive, CAP, 1)).astype(jnp.float32)
    own_ids = w * BLOCK_CH + slot_lane
    row_ids = lax.broadcasted_iota(jnp.int32, (SHARE, BLOCK_CH), 0)
    keeps = []
    for k in range(NY):
        ids = jnp.zeros((SHARE, BLOCK_CH), jnp.int32)
        for i in range(SHARE):
            ids = jnp.where(row_ids == i, source_index[k * SHARE + i], ids)
        keeps.append(jnp.where(ids != own_ids, alive, 0.0))
    last = HOPS - 1
    arrived(right_in.at[last - 1], right_recv.at[last - 1])
    arrived(left_in.at[last - 1], left_recv.at[last - 1])
    for i in range(TAILS):
        arrived(tail(right_in.at[last], i), right_recv.at[last + i])
        arrived(tail(left_in.at[last], i), left_recv.at[last + i])

        @pl.loop(i * TAIL, (i + 1) * TAIL)
        def _(f):
            for k in range(NY):
                total = sums[NZ - 1, k, f].astype(jnp.float32)
                from_right = right_in[last - k // 2, k % 2, f]
                from_left = left_in[last - 1 + k // 2, k % 2, f]
                total = total + from_right.astype(jnp.float32) + from_left.astype(jnp.float32)
                masked[k, f] = (total * keeps[k]).astype(jnp.bfloat16)

        part = pl.ds(i * TAIL, TAIL)
        for t in range(1, NY):
            to = lax.rem(y + t, NY)
            pltpu.make_async_remote_copy(
                src_ref=masked.at[to, part],
                dst_ref=quarters.at[y, part],
                send_sem=y_send,
                recv_sem=y_recv,
                device_id=(w, to),
                device_id_type=MESH,
            ).start()
    pltpu.make_async_copy(masked.at[y], quarters.at[y], y_recv).start()
    arrived(quarters, y_recv)
    for n in range(NY):
        out[n * FC : (n + 1) * FC] = quarters[n]

    arrived(masked.at[pl.ds(0, NY - 1)], y_send)
    arrived(source_in.at[pl.ds(0, PLANE - 1)], source_send)
    for group, (first, number) in enumerate(GROUPS):
        arrived(incoming.at[pl.ds(first, number), pl.ds(0, PLANE - 1)], send_sem.at[group])
    for m in range(HOPS - 1):
        arrived(half(*right[m]), right_send.at[m])
        arrived(half(*left[m]), left_send.at[m])
    for i in range(TAILS):
        arrived(tail(half(*right[last]), i), right_send.at[last + i])
        arrived(tail(half(*left[last]), i), left_send.at[last + i])

    @pl.loop(0, NZ)
    def _(plane):
        halo(plane).wait_send()


def masked_spectra(raw, filter_taps, dft, health, counts, source_index):
    bf16, f32 = jnp.bfloat16, jnp.float32
    dma = pltpu.SemaphoreType.DMA
    vmem = pl.BlockSpec(memory_space=pltpu.VMEM)
    whole = pl.BlockSpec(memory_space=pl.ANY)
    groups = len(GROUPS)
    return pl.pallas_call(
        spectra_kernel,
        out_shape=jax.ShapeDtypeStruct((F, SHARE, BLOCK_CH), bf16),
        in_specs=[whole, vmem, whole, whole, whole, whole],
        out_specs=vmem,
        scratch_shapes=[
            pltpu.VMEM((L, L), bf16),
            pltpu.VMEM((C // BLOCK_CH, BLOCK_CH), jnp.int32),
            pltpu.SMEM((C // BLOCK_CH,), jnp.int32),
            pltpu.SMEM((SRC,), jnp.int32),
            dma((4,)),
            pltpu.VMEM((STEPS, ROW, STEP_RAW), bf16),
            pltpu.VMEM((HALO, C), bf16),
            pltpu.VMEM((HALO, C // 2), bf16),
            pltpu.VMEM((HALO, C // 2), bf16),
            pltpu.VMEM((L, ROW), bf16),
            pltpu.VMEM((8, BLOCK_CH), f32),
            pltpu.VMEM((STEPS, L, STEP_CH), f32),
            pltpu.VMEM((F, BLOCK_CH), f32),
            pltpu.VMEM((1, BLOCK_CH), f32),
            pltpu.VMEM((2 * F, BLOCK_CH), f32),
            pltpu.VMEM((NZ, NXC, F, BLOCK_CH), bf16),
            pltpu.VMEM((NZ, PLANE, FC, BLOCK_CH), bf16),
            pltpu.VMEM((F, BLOCK_CH), bf16),
            pltpu.VMEM((PLANE, FC, BLOCK_CH), bf16),
            pltpu.VMEM((FC, PLANE, BLOCK_CH), bf16),
            pltpu.VMEM((FC, PLANE, BLOCK_CH), bf16),
            pltpu.VMEM((NZ, NY, FC, SHARE, BLOCK_CH), bf16),
            pltpu.VMEM((HOPS, 2, FC, SHARE, BLOCK_CH), bf16),
            pltpu.VMEM((HOPS, 2, FC, SHARE, BLOCK_CH), bf16),
            pltpu.VMEM((NY, FC, SHARE, BLOCK_CH), bf16),
            pltpu.VMEM((NY, FC, SHARE, BLOCK_CH), bf16),
            dma((STEPS,)),
            dma,
            dma((NZ,)),
            dma((NZ,)),
            dma((groups,)),
            dma((groups,)),
            dma,
            dma,
            dma((HOPS + TAILS - 1,)),
            dma((HOPS + TAILS - 1,)),
            dma((HOPS + TAILS - 1,)),
            dma((HOPS + TAILS - 1,)),
            dma,
            dma,
        ],
        compiler_params=pltpu.CompilerParams(
            collective_id=0, has_side_effects=True, vmem_limit_bytes=60 << 20
        ),
        name="masked_spectra",
    )(raw, filter_taps, dft, health, counts, source_index)


def lag_kernel(masked, table, out, by_source):
    step = pl.program_id(0)

    @pl.when(step == 0)
    def _():
        by_source[...] = jnp.swapaxes(masked[...], 0, 1)

    factor = 1.0 / math.sqrt(WIDE * NY * F)
    for k in range(out.shape[0]):
        turned = by_source[step * out.shape[0] + k].T
        out[k, :CAP] = factor * (
            jnp.dot(turned[:CAP], table[0], preferred_element_type=jnp.float32)
            + jnp.dot(turned[CAP:], table[1], preferred_element_type=jnp.float32)
        )
        out[k, CAP:] = jnp.zeros((BLOCK_CH - CAP, L), jnp.float32)


def correlations(masked, table):
    part = 4
    return pl.pallas_call(
        lag_kernel,
        grid=(SHARE // part,),
        out_shape=jax.ShapeDtypeStruct((SHARE, BLOCK_CH, L), jnp.float32),
        in_specs=[
            pl.BlockSpec((F, SHARE, BLOCK_CH), lambda i: (0, 0, 0)),
            pl.BlockSpec((2, F, L), lambda i: (0, 0, 0)),
        ],
        out_specs=pl.BlockSpec((part, BLOCK_CH, L), lambda i: (i, 0, 0)),
        scratch_shapes=[pltpu.VMEM((SHARE, F, BLOCK_CH), jnp.bfloat16)],
        compiler_params=pltpu.CompilerParams(vmem_limit_bytes=60 << 20),
        name="correlations",
    )(masked, table)


def body(raw_record, filter_taps, health_mask, counts, source_index):
    masked = masked_spectra(
        raw_record,
        filter_taps.reshape(1, K),
        jnp.asarray(dft_table()),
        health_mask.reshape(C // BLOCK_CH, BLOCK_CH),
        counts,
        source_index,
    )
    return correlations(masked, jnp.asarray(lag_table()))


def solution(mesh):
    placed = (P("narrow", "wide", None), P(), P(), P(), P())
    return jax.shard_map(
        body, mesh=mesh, in_specs=placed, out_specs=P("narrow", "wide", None), check_vma=False
    )
```

```python
import functools
import math

import jax
import jax.numpy as jnp
import numpy as np
from jax import lax
from jax.experimental import pallas as pl
from jax.experimental.pallas import tpu as pltpu
from jax.sharding import PartitionSpec as P

C = 8192
BLOCK_CH = 128
CAP = 64
Q = 2
L = 256
F = 128
K = 32
SRC = 64
NZ, NX, NC, NY = 8, 4, 2, 4
WIDE = NZ * NX * NC
HALO = 32
NXC = NX * NC
PLANE = NXC * NY
FC = F // NY
GROUP = 16
SHARE = SRC // NY
STEPS = NZ
STEP_RAW = C // STEPS
STEP_CH = STEP_RAW // 2
ROW = L * Q
MESH = pl.DeviceIdType.MESH
Z_ORDER = (4, 3, 5, 2, 6, 1, 7, 0)
GROUPS = ((0, 1), (1, 2), (3, 2), (5, 3))
HOPS = 7
TAIL = 8
TAILS = FC // TAIL


def dft_table():
    phases = np.arange(1, F + 1)[:, None] * np.arange(L)[None, :] % L
    angles = phases.astype(np.float32) * np.float32(2.0 * math.pi / L)
    return np.concatenate([np.cos(angles), -np.sin(angles)], axis=0).astype(jnp.bfloat16)


def lag_table():
    phases = np.arange(1, F + 1)[:, None] * (np.arange(L)[None, :] - L // 2) % L
    angles = phases.astype(np.float32) * np.float32(2.0 * math.pi / L)
    return np.stack([np.cos(angles), -np.sin(angles)], axis=0).astype(jnp.bfloat16)


def lanes(shape):
    return lax.broadcasted_iota(jnp.int32, shape, len(shape) - 1)


def paired(even, odd):
    return jnp.where(lanes(even.shape) < CAP, even, pltpu.roll(odd, CAP, 1))


def step_plane(step, z):
    distance = jnp.int32(Z_ORDER[-1])
    for i, d in enumerate(Z_ORDER[:-1]):
        distance = jnp.where(step == i, jnp.int32(d), distance)
    return lax.rem(z + distance, NZ)


def spectra_kernel(
    raw, filter_taps, dft_hbm, health_hbm, counts_hbm, index_hbm, out,
    dft, health, counts, source_index, small_sem, slot_ids,
    samples, edge, edge_out, edge_in, taps, tap_row, decimated, level_acc, weight_acc, source_acc,
    outgoing, incoming, source_out, source_in, source_t, chan_t, sums, right_in, left_in,
    masked, quarters,
    raw_sem, edge_sem, halo_send, halo_recv, send_sem, recv_sem, source_send, source_recv,
    right_send, right_recv, left_send, left_recv, y_send, y_recv,
):
    w = lax.axis_index("wide")
    y = lax.axis_index("narrow")
    z, xc = w >> 3, w & (NXC - 1)
    me = xc * NY + y

    def peer(t):
        other = (me + t) & (PLANE - 1)
        return other >> 2, other & (NY - 1)

    edge_copy = pltpu.make_async_copy(raw.at[0, pl.ds(ROW - HALO, HALO)], edge, edge_sem)
    edge_copy.start()
    small = [
        pltpu.make_async_copy(src, dst, small_sem.at[i])
        for i, (src, dst) in enumerate(
            (
                (index_hbm, source_index),
                (counts_hbm, counts),
                (health_hbm, health),
                (dft_hbm, dft),
            )
        )
    ]
    for copy in small:
        copy.start()

    def raw_copy(step):
        at = pl.multiple_of(step_plane(step, z) * STEP_RAW, STEP_RAW)
        return pltpu.make_async_copy(
            raw.at[0, :, pl.ds(at, STEP_RAW)], samples.at[step], raw_sem.at[step]
        )

    @pl.loop(0, STEPS)
    def _(step):
        raw_copy(step).start()

    barrier = pltpu.get_barrier_semaphore()

    def greet(wide, narrow):
        pl.semaphore_signal(barrier, inc=1, device_id=(wide, narrow), device_id_type=MESH)

    z_right, z_left = lax.rem(w + NXC, WIDE), lax.rem(w + WIDE - NXC, WIDE)
    after, before = lax.rem(w + 1, WIDE), lax.rem(w + WIDE - 1, WIDE)
    for wide in (after, before, z_right, z_left):
        greet(wide, y)

    @pl.loop(1, PLANE)
    def _(t):
        to_xc, to_y = peer(t)
        greet(z * NXC + to_xc, to_y)

    edge_copy.wait()
    for b in range(C // BLOCK_CH // 2):
        at = 2 * b * BLOCK_CH
        pair = edge[:, at : at + 2 * BLOCK_CH].astype(jnp.float32)
        edge_out[:, b * BLOCK_CH : (b + 1) * BLOCK_CH] = paired(
            pair[:, :BLOCK_CH], pair[:, BLOCK_CH:]
        ).astype(jnp.bfloat16)

    pl.semaphore_wait(barrier, PLANE - 1 + 4)

    def halo(plane):
        columns = pl.ds(pl.multiple_of(plane * STEP_CH, STEP_CH), STEP_CH)
        return pltpu.make_async_remote_copy(
            src_ref=edge_out.at[:, columns],
            dst_ref=edge_in.at[:, columns],
            send_sem=halo_send.at[plane],
            recv_sem=halo_recv.at[plane],
            device_id=(after, y),
            device_id_type=MESH,
        )

    @pl.loop(0, STEPS)
    def _(step):
        halo(step_plane(step, z)).start()

    tap_row[...] = jnp.zeros_like(tap_row)
    tap_row[0:1, :K] = filter_taps[...].astype(jnp.float32)
    tap_ids = lax.broadcasted_iota(jnp.int32, (BLOCK_CH, ROW), 0)
    place = (lanes((BLOCK_CH, ROW)) + tap_ids == 1) | (lanes((BLOCK_CH, ROW)) + tap_ids == ROW + 1)
    first_row = jnp.dot(
        tap_row[...].astype(jnp.bfloat16),
        jnp.where(place, 1.0, 0.0).astype(jnp.bfloat16),
        preferred_element_type=jnp.float32,
    )
    circular = pltpu.roll(
        jnp.broadcast_to(first_row[0:1, :], (L, ROW)), 0, 1, stride=Q, stride_axis=0
    )
    rows = lax.broadcasted_iota(jnp.int32, (L, ROW), 0)
    inside = lanes((L, ROW)) <= Q * rows + 1
    taps[...] = jnp.where(inside, circular, 0.0).astype(jnp.bfloat16)
    halo_taps = jnp.where(inside[:16], 0.0, circular[:16])[:, ROW - BLOCK_CH :]
    halo_taps = pltpu.roll(jnp.where(w == 0, 0.0, halo_taps), HALO, 1)[:, :HALO]
    halo_taps = halo_taps.astype(jnp.bfloat16)

    lane = lanes((1, BLOCK_CH))
    slot_lane = lane & (CAP - 1)
    for copy in small:
        copy.wait()
    source_row = jnp.zeros((1, BLOCK_CH), jnp.int32)
    for k in range(SRC):
        source_row = jnp.where(slot_lane == k, source_index[k], source_row)

    slots = lax.broadcasted_iota(jnp.int32, (STEP_CH, BLOCK_CH), 0)
    slot_ids[...] = 2 * slots - (slots & (CAP - 1))
    level_acc[...] = jnp.zeros_like(level_acc)
    weight_acc[...] = jnp.zeros_like(weight_acc)
    source_acc[...] = jnp.zeros_like(source_acc)

    @pl.loop(0, STEPS)
    def _(step):
        raw_copy(step).wait()
        d = jnp.dot(taps[...], samples[step], preferred_element_type=jnp.float32)
        for p in range(NX):
            at = 2 * p * BLOCK_CH
            decimated[step, :, p * BLOCK_CH : (p + 1) * BLOCK_CH] = paired(
                d[:, at : at + BLOCK_CH], d[:, at + BLOCK_CH : at + 2 * BLOCK_CH]
            )

    def spectra_step(step):
        plane = step_plane(step, z)
        first = plane * NX
        at = pl.multiple_of(plane * STEP_CH, STEP_CH)
        halo(plane).wait_recv()
        head = jnp.dot(
            halo_taps, edge_in[:, pl.ds(at, STEP_CH)], preferred_element_type=jnp.float32
        )
        d = decimated[step]
        d = jnp.concatenate([d[:16] + head, d[16:]], axis=0)
        scaling = lax.rsqrt(jnp.sum(d * d, axis=0, keepdims=True) * (1.0 / L) + 1e-06)
        normed = (d * scaling).astype(jnp.bfloat16)
        spectra = jnp.dot(dft[...], normed, preferred_element_type=jnp.float32)
        total = level_acc[...]
        for p in range(NX):
            pair = first + p
            re = spectra[:F, p * BLOCK_CH : (p + 1) * BLOCK_CH]
            im = spectra[F:, p * BLOCK_CH : (p + 1) * BLOCK_CH]
            flags = paired(health[pl.ds(2 * pair, 1), :], health[pl.ds(2 * pair + 1, 1), :])
            count = jnp.where(lane < CAP, counts[2 * pair], counts[2 * pair + 1])
            weights = jnp.where(slot_lane < count, flags, 0).astype(jnp.float32)
            weight_acc[...] += weights
            total = total + (re * re + im * im) * weights
            low = lanes(re.shape) < CAP
            outgoing[step, 2 * p] = jnp.where(low, re, pltpu.roll(im, CAP, 1)).astype(jnp.bfloat16)
            outgoing[step, 2 * p + 1] = jnp.where(low, pltpu.roll(re, CAP, 1), im).astype(
                jnp.bfloat16
            )
        level_acc[...] = total
        chosen = jnp.where(slot_ids[...] == source_row - plane * STEP_RAW, 1.0, 0.0)
        chosen = chosen.astype(jnp.bfloat16)
        source_acc[...] += jnp.dot(
            spectra.astype(jnp.bfloat16), chosen, preferred_element_type=jnp.float32
        )

    def bins(to_y):
        return pl.ds(pl.multiple_of(to_y * FC, FC), FC)

    def send_group(group):
        slots = pl.ds(*GROUPS[group])

        @pl.loop(1, PLANE)
        def _(t):
            to_xc, to_y = peer(t)
            pltpu.make_async_remote_copy(
                src_ref=outgoing.at[slots, to_xc, bins(to_y)],
                dst_ref=incoming.at[slots, me],
                send_sem=send_sem.at[group],
                recv_sem=recv_sem.at[group],
                device_id=(z * NXC + to_xc, to_y),
                device_id_type=MESH,
            ).start()

        pltpu.make_async_copy(
            outgoing.at[slots, xc, bins(y)], incoming.at[slots, me], recv_sem.at[group]
        ).start()

    def arrived(view, sem):
        pltpu.make_async_copy(view, view, sem).wait()

    spectra_step(0)
    send_group(0)

    @pl.loop(1, STEPS)
    def _(step):
        spectra_step(step)

    levels = jnp.sum(level_acc[...], axis=1, keepdims=True) / jnp.sum(weight_acc[...]) + 1e-06
    picked = source_acc[...]
    picked = jnp.where(lanes((F, BLOCK_CH)) < SRC, picked[:F], picked[F:])
    source_out[...] = (picked / levels).astype(jnp.bfloat16)

    @pl.loop(1, PLANE)
    def _(t):
        to_xc, to_y = peer(t)
        pltpu.make_async_remote_copy(
            src_ref=source_out.at[bins(to_y)],
            dst_ref=source_in.at[me],
            send_sem=source_send,
            recv_sem=source_recv,
            device_id=(z * NXC + to_xc, to_y),
            device_id_type=MESH,
        ).start()

    pltpu.make_async_copy(source_out.at[bins(y)], source_in.at[me], source_recv).start()
    send_group(1)

    def by_bin(held, turned):
        for f in range(FC // GROUP):
            for q in range(PLANE // GROUP):
                turned[f * GROUP : (f + 1) * GROUP, q * GROUP : (q + 1) * GROUP, :] = jnp.swapaxes(
                    held[q * GROUP : (q + 1) * GROUP, f * GROUP : (f + 1) * GROUP, :], 0, 1
                )

    arrived(incoming.at[pl.ds(*GROUPS[0])], recv_sem.at[0])
    by_bin(incoming.at[0], chan_t)
    arrived(source_in, source_recv)
    by_bin(source_in, source_t)
    sign = jnp.where(lanes((SRC, BLOCK_CH)) < CAP, 1.0, -1.0)

    def cross_slots(group):
        first, number = GROUPS[group]
        if first > 0:
            arrived(incoming.at[pl.ds(first, number)], recv_sem.at[group])
        for slot in range(first, first + number):
            if slot > 0:
                by_bin(incoming.at[slot], chan_t)

            @pl.loop(0, FC // 8)
            def _(g, slot=slot):
                for i in range(8):
                    f = g * 8 + i
                    product = lax.dot_general(
                        source_t[f], chan_t[f], (((0,), (0,)), ((), ())),
                        preferred_element_type=jnp.float32,
                    )
                    both = product[:SRC] + sign * pltpu.roll(product[SRC:], CAP, 1)
                    both = both.astype(jnp.bfloat16)
                    for k in range(NY):
                        sums[slot, k, f] = both[k * SHARE : (k + 1) * SHARE]

    right = ((0, 0), (1, 1), (1, 0), (3, 1), (3, 0), (5, 1), (5, 0))
    left = ((0, 1), (2, 0), (2, 1), (4, 0), (4, 1), (6, 0), (6, 1))

    def half(slot, part):
        return sums.at[slot, pl.ds(2 * part, 2)]

    def tail(ref, i):
        return ref.at[:, pl.ds(i * TAIL, TAIL)]

    def add_in(slot, part, landed):
        @pl.loop(0, FC)
        def _(f):
            for k in range(2):
                both = sums[slot, 2 * part + k, f].astype(jnp.float32)
                both = both + landed[k, f].astype(jnp.float32)
                sums[slot, 2 * part + k, f] = both.astype(jnp.bfloat16)

    def forward(m):
        for route, landed, sends, recvs, to in (
            (right, right_in, right_send, right_recv, z_right),
            (left, left_in, left_send, left_recv, z_left),
        ):
            slot, part = route[m]
            if m >= 2:
                arrived(landed.at[m - 2], recvs.at[m - 2])
                add_in(slot, part, landed.at[m - 2])
            if m < HOPS - 1:
                pieces = [(half(slot, part), landed.at[m], m)]
            else:
                pieces = [
                    (tail(half(slot, part), i), tail(landed.at[m], i), m + i) for i in range(TAILS)
                ]
            for src, dst, sem in pieces:
                pltpu.make_async_remote_copy(
                    src_ref=src,
                    dst_ref=dst,
                    send_sem=sends.at[sem],
                    recv_sem=recvs.at[sem],
                    device_id=(to, y),
                    device_id_type=MESH,
                ).start()

    cross_slots(0)
    forward(0)
    send_group(2)
    cross_slots(1)
    forward(1)
    forward(2)
    send_group(3)
    cross_slots(2)
    forward(3)
    forward(4)
    cross_slots(3)
    forward(5)
    forward(6)

    alive = jnp.where(slot_lane < counts[w], health[pl.ds(w, 1), :], 0)
    alive = jnp.where(lane < CAP, alive, pltpu.roll(alive, CAP, 1)).astype(jnp.float32)
    own_ids = w * BLOCK_CH + slot_lane
    row_ids = lax.broadcasted_iota(jnp.int32, (SHARE, BLOCK_CH), 0)
    keeps = []
    for k in range(NY):
        ids = jnp.zeros((SHARE, BLOCK_CH), jnp.int32)
        for i in range(SHARE):
            ids = jnp.where(row_ids == i, source_index[k * SHARE + i], ids)
        keeps.append(jnp.where(ids != own_ids, alive, 0.0))
    last = HOPS - 1
    arrived(right_in.at[last - 1], right_recv.at[last - 1])
    arrived(left_in.at[last - 1], left_recv.at[last - 1])
    for i in range(TAILS):
        arrived(tail(right_in.at[last], i), right_recv.at[last + i])
        arrived(tail(left_in.at[last], i), left_recv.at[last + i])

        @pl.loop(i * TAIL, (i + 1) * TAIL)
        def _(f):
            for k in range(NY):
                total = sums[NZ - 1, k, f].astype(jnp.float32)
                from_right = right_in[last - k // 2, k % 2, f]
                from_left = left_in[last - 1 + k // 2, k % 2, f]
                total = total + from_right.astype(jnp.float32) + from_left.astype(jnp.float32)
                masked[k, f] = (total * keeps[k]).astype(jnp.bfloat16)

        part = pl.ds(i * TAIL, TAIL)
        for t in range(1, NY):
            to = lax.rem(y + t, NY)
            pltpu.make_async_remote_copy(
                src_ref=masked.at[to, part],
                dst_ref=quarters.at[y, part],
                send_sem=y_send,
                recv_sem=y_recv,
                device_id=(w, to),
                device_id_type=MESH,
            ).start()
    pltpu.make_async_copy(masked.at[y], quarters.at[y], y_recv).start()
    arrived(quarters, y_recv)
    for n in range(NY):
        out[n * FC : (n + 1) * FC] = quarters[n]

    arrived(masked.at[pl.ds(0, NY - 1)], y_send)
    arrived(source_in.at[pl.ds(0, PLANE - 1)], source_send)
    for group, (first, number) in enumerate(GROUPS):
        arrived(incoming.at[pl.ds(first, number), pl.ds(0, PLANE - 1)], send_sem.at[group])
    for m in range(HOPS - 1):
        arrived(half(*right[m]), right_send.at[m])
        arrived(half(*left[m]), left_send.at[m])
    for i in range(TAILS):
        arrived(tail(half(*right[last]), i), right_send.at[last + i])
        arrived(tail(half(*left[last]), i), left_send.at[last + i])

    @pl.loop(0, NZ)
    def _(plane):
        halo(plane).wait_send()


def masked_spectra(raw, filter_taps, dft, health, counts, source_index):
    bf16, f32 = jnp.bfloat16, jnp.float32
    dma = pltpu.SemaphoreType.DMA
    vmem = pl.BlockSpec(memory_space=pltpu.VMEM)
    whole = pl.BlockSpec(memory_space=pl.ANY)
    groups = len(GROUPS)
    return pl.pallas_call(
        spectra_kernel,
        out_shape=jax.ShapeDtypeStruct((F, SHARE, BLOCK_CH), bf16),
        in_specs=[whole, vmem, whole, whole, whole, whole],
        out_specs=vmem,
        scratch_shapes=[
            pltpu.VMEM((L, L), bf16),
            pltpu.VMEM((C // BLOCK_CH, BLOCK_CH), jnp.int32),
            pltpu.SMEM((C // BLOCK_CH,), jnp.int32),
            pltpu.SMEM((SRC,), jnp.int32),
            dma((4,)),
            pltpu.VMEM((STEP_CH, BLOCK_CH), jnp.int32),
            pltpu.VMEM((STEPS, ROW, STEP_RAW), bf16),
            pltpu.VMEM((HALO, C), bf16),
            pltpu.VMEM((HALO, C // 2), bf16),
            pltpu.VMEM((HALO, C // 2), bf16),
            pltpu.VMEM((L, ROW), bf16),
            pltpu.VMEM((8, BLOCK_CH), f32),
            pltpu.VMEM((STEPS, L, STEP_CH), f32),
            pltpu.VMEM((F, BLOCK_CH), f32),
            pltpu.VMEM((1, BLOCK_CH), f32),
            pltpu.VMEM((2 * F, BLOCK_CH), f32),
            pltpu.VMEM((NZ, NXC, F, BLOCK_CH), bf16),
            pltpu.VMEM((NZ, PLANE, FC, BLOCK_CH), bf16),
            pltpu.VMEM((F, BLOCK_CH), bf16),
            pltpu.VMEM((PLANE, FC, BLOCK_CH), bf16),
            pltpu.VMEM((FC, PLANE, BLOCK_CH), bf16),
            pltpu.VMEM((FC, PLANE, BLOCK_CH), bf16),
            pltpu.VMEM((NZ, NY, FC, SHARE, BLOCK_CH), bf16),
            pltpu.VMEM((HOPS, 2, FC, SHARE, BLOCK_CH), bf16),
            pltpu.VMEM((HOPS, 2, FC, SHARE, BLOCK_CH), bf16),
            pltpu.VMEM((NY, FC, SHARE, BLOCK_CH), bf16),
            pltpu.VMEM((NY, FC, SHARE, BLOCK_CH), bf16),
            dma((STEPS,)),
            dma,
            dma((NZ,)),
            dma((NZ,)),
            dma((groups,)),
            dma((groups,)),
            dma,
            dma,
            dma((HOPS + TAILS - 1,)),
            dma((HOPS + TAILS - 1,)),
            dma((HOPS + TAILS - 1,)),
            dma((HOPS + TAILS - 1,)),
            dma,
            dma,
        ],
        compiler_params=pltpu.CompilerParams(
            collective_id=0, has_side_effects=True, vmem_limit_bytes=60 << 20
        ),
        name="masked_spectra",
    )(raw, filter_taps, dft, health, counts, source_index)


def lag_kernel(masked, table, out, by_source):
    step = pl.program_id(0)

    @pl.when(step == 0)
    def _():
        by_source[...] = jnp.swapaxes(masked[...], 0, 1)

    factor = 1.0 / math.sqrt(WIDE * NY * F)
    for k in range(out.shape[0]):
        turned = by_source[step * out.shape[0] + k].T
        out[k, :CAP] = factor * (
            jnp.dot(turned[:CAP], table[0], preferred_element_type=jnp.float32)
            + jnp.dot(turned[CAP:], table[1], preferred_element_type=jnp.float32)
        )
        out[k, CAP:] = jnp.zeros((BLOCK_CH - CAP, L), jnp.float32)


def correlations(masked, table):
    part = 8
    return pl.pallas_call(
        lag_kernel,
        grid=(SHARE // part,),
        out_shape=jax.ShapeDtypeStruct((SHARE, BLOCK_CH, L), jnp.float32),
        in_specs=[
            pl.BlockSpec((F, SHARE, BLOCK_CH), lambda i: (0, 0, 0)),
            pl.BlockSpec((2, F, L), lambda i: (0, 0, 0)),
        ],
        out_specs=pl.BlockSpec((part, BLOCK_CH, L), lambda i: (i, 0, 0)),
        scratch_shapes=[pltpu.VMEM((SHARE, F, BLOCK_CH), jnp.bfloat16)],
        compiler_params=pltpu.CompilerParams(vmem_limit_bytes=60 << 20),
        name="correlations",
    )(masked, table)


def body(raw_record, filter_taps, health_mask, counts, source_index):
    masked = masked_spectra(
        raw_record,
        filter_taps.reshape(1, K),
        jnp.asarray(dft_table()),
        health_mask.reshape(C // BLOCK_CH, BLOCK_CH),
        counts,
        source_index,
    )
    return correlations(masked, jnp.asarray(lag_table()))


def solution(mesh):
    placed = (P("narrow", "wide", None), P(), P(), P(), P())
    return jax.shard_map(
        body, mesh=mesh, in_specs=placed, out_specs=P("narrow", "wide", None), check_vma=False
    )
```

```python
import functools
import math

import jax
import jax.numpy as jnp
import numpy as np
from jax import lax
from jax.experimental import pallas as pl
from jax.experimental.pallas import tpu as pltpu
from jax.sharding import PartitionSpec as P

C = 8192
BLOCK_CH = 128
CAP = 64
Q = 2
L = 256
F = 128
K = 32
SRC = 64
NZ, NX, NC, NY = 8, 4, 2, 4
WIDE = NZ * NX * NC
HALO = 32
NXC = NX * NC
PLANE = NXC * NY
FC = F // NY
GROUP = 16
SHARE = SRC // NY
STEPS = NZ
STEP_RAW = C // STEPS
STEP_CH = STEP_RAW // 2
ROW = L * Q
MESH = pl.DeviceIdType.MESH
Z_ORDER = (4, 3, 5, 2, 6, 1, 7, 0)
GROUPS = ((0, 1), (1, 2), (3, 2), (5, 3))
HOPS = 7
TAIL = 8
TAILS = FC // TAIL


def dft_table():
    phases = np.arange(1, F + 1)[:, None] * np.arange(L)[None, :] % L
    angles = phases.astype(np.float32) * np.float32(2.0 * math.pi / L)
    return np.concatenate([np.cos(angles), -np.sin(angles)], axis=0).astype(jnp.bfloat16)


def lag_table():
    phases = np.arange(1, F + 1)[:, None] * (np.arange(L)[None, :] - L // 2) % L
    angles = phases.astype(np.float32) * np.float32(2.0 * math.pi / L)
    return np.stack([np.cos(angles), -np.sin(angles)], axis=0).astype(jnp.bfloat16)


def lanes(shape):
    return lax.broadcasted_iota(jnp.int32, shape, len(shape) - 1)


def paired(even, odd):
    return jnp.where(lanes(even.shape) < CAP, even, pltpu.roll(odd, CAP, 1))


def step_plane(step, z):
    distance = jnp.int32(Z_ORDER[-1])
    for i, d in enumerate(Z_ORDER[:-1]):
        distance = jnp.where(step == i, jnp.int32(d), distance)
    return lax.rem(z + distance, NZ)


def spectra_kernel(
    raw, filter_taps, dft_hbm, health_hbm, counts_hbm, index_hbm, out,
    dft, health, counts, source_index, small_sem, slot_ids,
    samples, edge, edge_out, edge_in, taps, tap_row, decimated, level_acc, weight_acc, source_acc,
    outgoing, incoming, source_out, source_in, source_t, chan_t, sums, right_in, left_in,
    masked, quarters,
    raw_sem, edge_sem, halo_send, halo_recv, send_sem, recv_sem, source_send, source_recv,
    right_send, right_recv, left_send, left_recv, y_send, y_recv,
):
    w = lax.axis_index("wide")
    y = lax.axis_index("narrow")
    z, xc = w >> 3, w & (NXC - 1)
    me = xc * NY + y

    def peer(t):
        other = (me + t) & (PLANE - 1)
        return other >> 2, other & (NY - 1)

    edge_copy = pltpu.make_async_copy(raw.at[0, pl.ds(ROW - HALO, HALO)], edge, edge_sem)
    edge_copy.start()
    small = [
        pltpu.make_async_copy(src, dst, small_sem.at[i])
        for i, (src, dst) in enumerate(
            (
                (index_hbm, source_index),
                (counts_hbm, counts),
                (health_hbm, health),
                (dft_hbm, dft),
            )
        )
    ]
    for copy in small:
        copy.start()

    def raw_copy(step):
        at = pl.multiple_of(step_plane(step, z) * STEP_RAW, STEP_RAW)
        return pltpu.make_async_copy(
            raw.at[0, :, pl.ds(at, STEP_RAW)], samples.at[step], raw_sem.at[step]
        )

    @pl.loop(0, STEPS)
    def _(step):
        raw_copy(step).start()

    barrier = pltpu.get_barrier_semaphore()

    def greet(wide, narrow):
        pl.semaphore_signal(barrier, inc=1, device_id=(wide, narrow), device_id_type=MESH)

    z_right, z_left = lax.rem(w + NXC, WIDE), lax.rem(w + WIDE - NXC, WIDE)
    after, before = lax.rem(w + 1, WIDE), lax.rem(w + WIDE - 1, WIDE)
    for wide in (after, before, z_right, z_left):
        greet(wide, y)

    @pl.loop(1, PLANE)
    def _(t):
        to_xc, to_y = peer(t)
        greet(z * NXC + to_xc, to_y)

    edge_copy.wait()
    for b in range(C // BLOCK_CH // 2):
        at = 2 * b * BLOCK_CH
        pair = edge[:, at : at + 2 * BLOCK_CH].astype(jnp.float32)
        edge_out[:, b * BLOCK_CH : (b + 1) * BLOCK_CH] = paired(
            pair[:, :BLOCK_CH], pair[:, BLOCK_CH:]
        ).astype(jnp.bfloat16)

    pl.semaphore_wait(barrier, PLANE - 1 + 4)

    def halo(plane):
        columns = pl.ds(pl.multiple_of(plane * STEP_CH, STEP_CH), STEP_CH)
        return pltpu.make_async_remote_copy(
            src_ref=edge_out.at[:, columns],
            dst_ref=edge_in.at[:, columns],
            send_sem=halo_send.at[plane],
            recv_sem=halo_recv.at[plane],
            device_id=(after, y),
            device_id_type=MESH,
        )

    @pl.loop(0, STEPS)
    def _(step):
        halo(step_plane(step, z)).start()

    tap_row[...] = jnp.zeros_like(tap_row)
    tap_row[0:1, :K] = filter_taps[...].astype(jnp.float32)
    tap_ids = lax.broadcasted_iota(jnp.int32, (BLOCK_CH, ROW), 0)
    place = (lanes((BLOCK_CH, ROW)) + tap_ids == 1) | (lanes((BLOCK_CH, ROW)) + tap_ids == ROW + 1)
    first_row = jnp.dot(
        tap_row[...].astype(jnp.bfloat16),
        jnp.where(place, 1.0, 0.0).astype(jnp.bfloat16),
        preferred_element_type=jnp.float32,
    )
    circular = pltpu.roll(
        jnp.broadcast_to(first_row[0:1, :], (L, ROW)), 0, 1, stride=Q, stride_axis=0
    )
    rows = lax.broadcasted_iota(jnp.int32, (L, ROW), 0)
    inside = lanes((L, ROW)) <= Q * rows + 1
    taps[...] = jnp.where(inside, circular, 0.0).astype(jnp.bfloat16)
    halo_taps = jnp.where(inside[:16], 0.0, circular[:16])[:, ROW - BLOCK_CH :]
    halo_taps = pltpu.roll(jnp.where(w == 0, 0.0, halo_taps), HALO, 1)[:, :HALO]
    halo_taps = halo_taps.astype(jnp.bfloat16)

    lane = lanes((1, BLOCK_CH))
    slot_lane = lane & (CAP - 1)
    for copy in small:
        copy.wait()
    source_row = jnp.zeros((1, BLOCK_CH), jnp.int32)
    for k in range(SRC):
        source_row = jnp.where(slot_lane == k, source_index[k], source_row)

    slots = lax.broadcasted_iota(jnp.int32, (STEP_CH, BLOCK_CH), 0)
    slot_ids[...] = 2 * slots - (slots & (CAP - 1))
    level_acc[...] = jnp.zeros_like(level_acc)
    weight_acc[...] = jnp.zeros_like(weight_acc)
    source_acc[...] = jnp.zeros_like(source_acc)

    @pl.loop(0, STEPS)
    def _(step):
        raw_copy(step).wait()
        d = jnp.dot(taps[...], samples[step], preferred_element_type=jnp.float32)
        for p in range(NX):
            at = 2 * p * BLOCK_CH
            decimated[step, :, p * BLOCK_CH : (p + 1) * BLOCK_CH] = paired(
                d[:, at : at + BLOCK_CH], d[:, at + BLOCK_CH : at + 2 * BLOCK_CH]
            )

    def spectra_step(step):
        plane = step_plane(step, z)
        first = plane * NX
        at = pl.multiple_of(plane * STEP_CH, STEP_CH)
        halo(plane).wait_recv()
        head = jnp.dot(
            halo_taps, edge_in[:, pl.ds(at, STEP_CH)], preferred_element_type=jnp.float32
        )
        d = decimated[step]
        d = jnp.concatenate([d[:16] + head, d[16:]], axis=0)
        scaling = lax.rsqrt(jnp.sum(d * d, axis=0, keepdims=True) * (1.0 / L) + 1e-06)
        normed = (d * scaling).astype(jnp.bfloat16)
        spectra = jnp.dot(dft[...], normed, preferred_element_type=jnp.float32)
        total = level_acc[...]
        for p in range(NX):
            pair = first + p
            re = spectra[:F, p * BLOCK_CH : (p + 1) * BLOCK_CH]
            im = spectra[F:, p * BLOCK_CH : (p + 1) * BLOCK_CH]
            flags = paired(health[pl.ds(2 * pair, 1), :], health[pl.ds(2 * pair + 1, 1), :])
            count = jnp.where(lane < CAP, counts[2 * pair], counts[2 * pair + 1])
            weights = jnp.where(slot_lane < count, flags, 0).astype(jnp.float32)
            weight_acc[...] += weights
            total = total + (re * re + im * im) * weights
            low = lanes(re.shape) < CAP
            outgoing[step, 2 * p] = jnp.where(low, re, pltpu.roll(im, CAP, 1)).astype(jnp.bfloat16)
            outgoing[step, 2 * p + 1] = jnp.where(low, pltpu.roll(re, CAP, 1), im).astype(
                jnp.bfloat16
            )
        level_acc[...] = total
        chosen = jnp.where(slot_ids[...] == source_row - plane * STEP_RAW, 1.0, 0.0)
        chosen = chosen.astype(jnp.bfloat16)
        source_acc[...] += jnp.dot(
            spectra.astype(jnp.bfloat16), chosen, preferred_element_type=jnp.float32
        )

    def bins(to_y):
        return pl.ds(pl.multiple_of(to_y * FC, FC), FC)

    def send_group(group):
        slots = pl.ds(*GROUPS[group])

        @pl.loop(1, PLANE)
        def _(t):
            to_xc, to_y = peer(t)
            pltpu.make_async_remote_copy(
                src_ref=outgoing.at[slots, to_xc, bins(to_y)],
                dst_ref=incoming.at[slots, me],
                send_sem=send_sem.at[group],
                recv_sem=recv_sem.at[group],
                device_id=(z * NXC + to_xc, to_y),
                device_id_type=MESH,
            ).start()

        pltpu.make_async_copy(
            outgoing.at[slots, xc, bins(y)], incoming.at[slots, me], recv_sem.at[group]
        ).start()

    def arrived(view, sem):
        pltpu.make_async_copy(view, view, sem).wait()

    spectra_step(0)
    send_group(0)

    @pl.loop(1, STEPS)
    def _(step):
        spectra_step(step)

    levels = jnp.sum(level_acc[...], axis=1, keepdims=True) / jnp.sum(weight_acc[...]) + 1e-06
    picked = source_acc[...]
    picked = jnp.where(lanes((F, BLOCK_CH)) < SRC, picked[:F], picked[F:])
    source_out[...] = (picked / levels).astype(jnp.bfloat16)

    @pl.loop(1, PLANE)
    def _(t):
        to_xc, to_y = peer(t)
        pltpu.make_async_remote_copy(
            src_ref=source_out.at[bins(to_y)],
            dst_ref=source_in.at[me],
            send_sem=source_send,
            recv_sem=source_recv,
            device_id=(z * NXC + to_xc, to_y),
            device_id_type=MESH,
        ).start()

    pltpu.make_async_copy(source_out.at[bins(y)], source_in.at[me], source_recv).start()
    send_group(1)

    def by_bin(held, turned):
        for f in range(FC // GROUP):
            for q in range(PLANE // GROUP):
                turned[f * GROUP : (f + 1) * GROUP, q * GROUP : (q + 1) * GROUP, :] = jnp.swapaxes(
                    held[q * GROUP : (q + 1) * GROUP, f * GROUP : (f + 1) * GROUP, :], 0, 1
                )

    arrived(incoming.at[pl.ds(*GROUPS[0])], recv_sem.at[0])
    by_bin(incoming.at[0], chan_t)
    arrived(source_in, source_recv)
    by_bin(source_in, source_t)
    sign = jnp.where(lanes((SRC, BLOCK_CH)) < CAP, 1.0, -1.0)

    def cross_slots(group):
        first, number = GROUPS[group]
        if first > 0:
            arrived(incoming.at[pl.ds(first, number)], recv_sem.at[group])
        for slot in range(first, first + number):
            if slot > 0:
                by_bin(incoming.at[slot], chan_t)

            @pl.loop(0, FC // 8)
            def _(g, slot=slot):
                for i in range(8):
                    f = g * 8 + i
                    product = lax.dot_general(
                        source_t[f], chan_t[f], (((0,), (0,)), ((), ())),
                        preferred_element_type=jnp.float32,
                    )
                    both = product[:SRC] + sign * pltpu.roll(product[SRC:], CAP, 1)
                    both = both.astype(jnp.bfloat16)
                    for k in range(NY):
                        sums[slot, k, f] = both[k * SHARE : (k + 1) * SHARE]

    right = ((0, 0), (1, 1), (1, 0), (3, 1), (3, 0), (5, 1), (5, 0))
    left = ((0, 1), (2, 0), (2, 1), (4, 0), (4, 1), (6, 0), (6, 1))

    def half(slot, part):
        return sums.at[slot, pl.ds(2 * part, 2)]

    def tail(ref, i):
        return ref.at[:, pl.ds(i * TAIL, TAIL)]

    def add_in(slot, part, landed):
        @pl.loop(0, FC)
        def _(f):
            for k in range(2):
                both = sums[slot, 2 * part + k, f].astype(jnp.float32)
                both = both + landed[k, f].astype(jnp.float32)
                sums[slot, 2 * part + k, f] = both.astype(jnp.bfloat16)

    def forward(m):
        for route, landed, sends, recvs, to in (
            (right, right_in, right_send, right_recv, z_right),
            (left, left_in, left_send, left_recv, z_left),
        ):
            slot, part = route[m]
            if m >= 2:
                arrived(landed.at[m - 2], recvs.at[m - 2])
                add_in(slot, part, landed.at[m - 2])
            if m < HOPS - 1:
                pieces = [(half(slot, part), landed.at[m], m)]
            else:
                pieces = [
                    (tail(half(slot, part), i), tail(landed.at[m], i), m + i) for i in range(TAILS)
                ]
            for src, dst, sem in pieces:
                pltpu.make_async_remote_copy(
                    src_ref=src,
                    dst_ref=dst,
                    send_sem=sends.at[sem],
                    recv_sem=recvs.at[sem],
                    device_id=(to, y),
                    device_id_type=MESH,
                ).start()

    cross_slots(0)
    forward(0)
    send_group(2)
    cross_slots(1)
    forward(1)
    forward(2)
    send_group(3)
    cross_slots(2)
    forward(3)
    forward(4)
    cross_slots(3)
    forward(5)
    forward(6)

    alive = jnp.where(slot_lane < counts[w], health[pl.ds(w, 1), :], 0)
    alive = jnp.where(lane < CAP, alive, pltpu.roll(alive, CAP, 1)).astype(jnp.float32)
    own_ids = w * BLOCK_CH + slot_lane
    row_ids = lax.broadcasted_iota(jnp.int32, (SHARE, BLOCK_CH), 0)
    keeps = []
    for k in range(NY):
        ids = jnp.zeros((SHARE, BLOCK_CH), jnp.int32)
        for i in range(SHARE):
            ids = jnp.where(row_ids == i, source_index[k * SHARE + i], ids)
        keeps.append(jnp.where(ids != own_ids, alive, 0.0))
    last = HOPS - 1
    arrived(right_in.at[last - 1], right_recv.at[last - 1])
    arrived(left_in.at[last - 1], left_recv.at[last - 1])
    for i in range(TAILS):
        arrived(tail(right_in.at[last], i), right_recv.at[last + i])
        arrived(tail(left_in.at[last], i), left_recv.at[last + i])

        @pl.loop(i * TAIL, (i + 1) * TAIL)
        def _(f):
            for k in range(NY):
                total = sums[NZ - 1, k, f].astype(jnp.float32)
                from_right = right_in[last - k // 2, k % 2, f]
                from_left = left_in[last - 1 + k // 2, k % 2, f]
                total = total + from_right.astype(jnp.float32) + from_left.astype(jnp.float32)
                masked[k, f] = (total * keeps[k]).astype(jnp.bfloat16)

        part = pl.ds(i * TAIL, TAIL)
        for t in range(1, NY):
            to = lax.rem(y + t, NY)
            pltpu.make_async_remote_copy(
                src_ref=masked.at[to, part],
                dst_ref=quarters.at[y, part],
                send_sem=y_send,
                recv_sem=y_recv,
                device_id=(w, to),
                device_id_type=MESH,
            ).start()
    pltpu.make_async_copy(masked.at[y], quarters.at[y], y_recv).start()
    arrived(quarters, y_recv)
    results = [
        pltpu.make_async_copy(quarters.at[n], out.at[pl.ds(n * FC, FC)], small_sem.at[n])
        for n in range(NY)
    ]
    for copy in results:
        copy.start()

    arrived(masked.at[pl.ds(0, NY - 1)], y_send)
    arrived(source_in.at[pl.ds(0, PLANE - 1)], source_send)
    for group, (first, number) in enumerate(GROUPS):
        arrived(incoming.at[pl.ds(first, number), pl.ds(0, PLANE - 1)], send_sem.at[group])
    for m in range(HOPS - 1):
        arrived(half(*right[m]), right_send.at[m])
        arrived(half(*left[m]), left_send.at[m])
    for i in range(TAILS):
        arrived(tail(half(*right[last]), i), right_send.at[last + i])
        arrived(tail(half(*left[last]), i), left_send.at[last + i])

    @pl.loop(0, NZ)
    def _(plane):
        halo(plane).wait_send()

    for copy in results:
        copy.wait()


def masked_spectra(raw, filter_taps, dft, health, counts, source_index):
    bf16, f32 = jnp.bfloat16, jnp.float32
    dma = pltpu.SemaphoreType.DMA
    vmem = pl.BlockSpec(memory_space=pltpu.VMEM)
    whole = pl.BlockSpec(memory_space=pl.ANY)
    groups = len(GROUPS)
    return pl.pallas_call(
        spectra_kernel,
        out_shape=jax.ShapeDtypeStruct((F, SHARE, BLOCK_CH), bf16),
        in_specs=[whole, vmem, whole, whole, whole, whole],
        out_specs=whole,
        scratch_shapes=[
            pltpu.VMEM((L, L), bf16),
            pltpu.VMEM((C // BLOCK_CH, BLOCK_CH), jnp.int32),
            pltpu.SMEM((C // BLOCK_CH,), jnp.int32),
            pltpu.SMEM((SRC,), jnp.int32),
            dma((4,)),
            pltpu.VMEM((STEP_CH, BLOCK_CH), jnp.int32),
            pltpu.VMEM((STEPS, ROW, STEP_RAW), bf16),
            pltpu.VMEM((HALO, C), bf16),
            pltpu.VMEM((HALO, C // 2), bf16),
            pltpu.VMEM((HALO, C // 2), bf16),
            pltpu.VMEM((L, ROW), bf16),
            pltpu.VMEM((8, BLOCK_CH), f32),
            pltpu.VMEM((STEPS, L, STEP_CH), f32),
            pltpu.VMEM((F, BLOCK_CH), f32),
            pltpu.VMEM((1, BLOCK_CH), f32),
            pltpu.VMEM((2 * F, BLOCK_CH), f32),
            pltpu.VMEM((NZ, NXC, F, BLOCK_CH), bf16),
            pltpu.VMEM((NZ, PLANE, FC, BLOCK_CH), bf16),
            pltpu.VMEM((F, BLOCK_CH), bf16),
            pltpu.VMEM((PLANE, FC, BLOCK_CH), bf16),
            pltpu.VMEM((FC, PLANE, BLOCK_CH), bf16),
            pltpu.VMEM((FC, PLANE, BLOCK_CH), bf16),
            pltpu.VMEM((NZ, NY, FC, SHARE, BLOCK_CH), bf16),
            pltpu.VMEM((HOPS, 2, FC, SHARE, BLOCK_CH), bf16),
            pltpu.VMEM((HOPS, 2, FC, SHARE, BLOCK_CH), bf16),
            pltpu.VMEM((NY, FC, SHARE, BLOCK_CH), bf16),
            pltpu.VMEM((NY, FC, SHARE, BLOCK_CH), bf16),
            dma((STEPS,)),
            dma,
            dma((NZ,)),
            dma((NZ,)),
            dma((groups,)),
            dma((groups,)),
            dma,
            dma,
            dma((HOPS + TAILS - 1,)),
            dma((HOPS + TAILS - 1,)),
            dma((HOPS + TAILS - 1,)),
            dma((HOPS + TAILS - 1,)),
            dma,
            dma,
        ],
        compiler_params=pltpu.CompilerParams(
            collective_id=0, has_side_effects=True, vmem_limit_bytes=60 << 20
        ),
        name="masked_spectra",
    )(raw, filter_taps, dft, health, counts, source_index)


def lag_kernel(masked, table, out, by_source):
    step = pl.program_id(0)

    @pl.when(step == 0)
    def _():
        by_source[...] = jnp.swapaxes(masked[...], 0, 1)

    factor = 1.0 / math.sqrt(WIDE * NY * F)
    for k in range(out.shape[0]):
        turned = by_source[step * out.shape[0] + k].T
        out[k, :CAP] = factor * (
            jnp.dot(turned[:CAP], table[0], preferred_element_type=jnp.float32)
            + jnp.dot(turned[CAP:], table[1], preferred_element_type=jnp.float32)
        )
        out[k, CAP:] = jnp.zeros((BLOCK_CH - CAP, L), jnp.float32)


def correlations(masked, table):
    part = 8
    return pl.pallas_call(
        lag_kernel,
        grid=(SHARE // part,),
        out_shape=jax.ShapeDtypeStruct((SHARE, BLOCK_CH, L), jnp.float32),
        in_specs=[
            pl.BlockSpec((F, SHARE, BLOCK_CH), lambda i: (0, 0, 0)),
            pl.BlockSpec((2, F, L), lambda i: (0, 0, 0)),
        ],
        out_specs=pl.BlockSpec((part, BLOCK_CH, L), lambda i: (i, 0, 0)),
        scratch_shapes=[pltpu.VMEM((SHARE, F, BLOCK_CH), jnp.bfloat16)],
        compiler_params=pltpu.CompilerParams(vmem_limit_bytes=60 << 20),
        name="correlations",
    )(masked, table)


def body(raw_record, filter_taps, health_mask, counts, source_index):
    masked = masked_spectra(
        raw_record,
        filter_taps.reshape(1, K),
        jnp.asarray(dft_table()),
        health_mask.reshape(C // BLOCK_CH, BLOCK_CH),
        counts,
        source_index,
    )
    return correlations(masked, jnp.asarray(lag_table()))


def solution(mesh):
    placed = (P("narrow", "wide", None), P(), P(), P(), P())
    return jax.shard_map(
        body, mesh=mesh, in_specs=placed, out_specs=P("narrow", "wide", None), check_vma=False
    )
```
